32 devices in a mesh: head: 16 (over z, x, core), ctx: 2 (over y).
Axes of the slice: x: 2, y: 2, z: 4, core: 2. Of those that a mesh axis runs over, the one named last changes fastest.
Arguments:
- queries: bfloat16 [4096, 8192], P('ctx', 'head'), may hold values from -6 to 6
- keys: bfloat16 [128, 512], P(('head', 'ctx')), may hold values from -6 to 6
- values: bfloat16 [128, 512], P(('head', 'ctx')), may hold values from -6 to 6
- outputs: bfloat16 [4096, 8192], P('ctx', 'head'), may hold values from -6 to 6
- dout: bfloat16 [4096, 8192], P(('ctx', 'head')), may hold values from -24 to 24
- lse: float32 [64, 4096], P('head', 'ctx'), may hold values from 6.5 to 8.5
Outputs:
- dq: bfloat16 [4096, 8192], P('ctx', 'head')
- dk: bfloat16 [128, 512], P(('head', 'ctx'))
- dv: bfloat16 [128, 512], P(('head', 'ctx'))
The draws below stay inside these ranges and needn't reach their ends.
All inputs are finite; a program needn't handle non-finite values.
Results may differ from the reference program's by a relative error of at most 0.0052.
Values may be sent and summed in bfloat16 or wider, within the bound.
No kernel may reach another device: no remote copies, remote signals or barrier semaphores. Data moves between devices by JAX's collectives and lax.ppermute only.
A program may use at most 128 MiB of HBM per device.

```python
import jax
import jax.numpy as jnp
from jax import lax

QUERY_HEADS = 64
KEY_VALUE_HEADS = 4
HEAD_SIZE = 128
SQ = 4096
TOTAL_KEYS = 128


def steps_of(stream_key, dims, split, least, top_value):
    def one(dim, parts):
        heights = jax.random.uniform(jax.random.fold_in(jax.random.fold_in(stream_key, 6), dim), (parts,), jnp.float32, least / len(split), top_value / len(split))
        return jnp.repeat(jnp.exp(heights), dims[dim] // parts).reshape((-1,) + (1,) * (len(dims) - dim - 1))

    level = one(*split[0])
    for cut in split[1:]:
        level = level * one(*cut)
    return level


def scatter_about(key, extent, spread, reach, shards=(), kind=jnp.bfloat16):
    values = spread * jax.random.normal(key, extent, jnp.float32)
    if shards:
        values = values * steps_of(key, extent, shards, -0.22, 0.18)
    return jnp.clip(values, -reach, reach).astype(kind)


def setup_inputs(seed: int = 0) -> dict:
    key_of = jax.random.split(jax.random.key(seed), 7)
    return {
        "queries": scatter_about(key_of[0], (SQ, QUERY_HEADS * HEAD_SIZE), 1.0, 6.0, ((0, 2), (1, 16))),
        "keys": scatter_about(key_of[1], (TOTAL_KEYS, KEY_VALUE_HEADS * HEAD_SIZE), 1.0, 6.0, ((0, 32),)),
        "values": scatter_about(key_of[2], (TOTAL_KEYS, KEY_VALUE_HEADS * HEAD_SIZE), 1.0, 6.0, ((0, 32),)),
        "outputs": scatter_about(key_of[3], (SQ, QUERY_HEADS * HEAD_SIZE), 1.0, 6.0, ((0, 2), (1, 16))),
        "dout": scatter_about(key_of[4], (SQ, QUERY_HEADS * HEAD_SIZE), 4.0, 24.0, ((0, 32),)),
        "lse": jnp.clip(6.5 + 2.0 * jax.random.uniform(key_of[5], (QUERY_HEADS, SQ), jnp.float32) ** steps_of(key_of[5], (QUERY_HEADS, SQ), ((0, 16), (1, 2)), -0.2, 0.2), 6.5, 8.5),
    }


def reference(queries, keys, values, outputs, dout, lse):
    factor = HEAD_SIZE ** -0.5
    heads_per_group = QUERY_HEADS // KEY_VALUE_HEADS
    dq_parts = []
    dk_parts = []
    dv_parts = []
    for key_value_index in range(KEY_VALUE_HEADS):
        key_group = keys[:, key_value_index * HEAD_SIZE:(key_value_index + 1) * HEAD_SIZE]
        value_group = values[:, key_value_index * HEAD_SIZE:(key_value_index + 1) * HEAD_SIZE]
        first = key_value_index * heads_per_group
        span = slice(first * HEAD_SIZE, (first + heads_per_group) * HEAD_SIZE)
        q_stack = queries[:, span].reshape(SQ, heads_per_group, HEAD_SIZE).transpose(1, 0, 2)
        o_stack = outputs[:, span].reshape(SQ, heads_per_group, HEAD_SIZE).transpose(1, 0, 2)
        d_stack = dout[:, span].reshape(SQ, heads_per_group, HEAD_SIZE).transpose(1, 0, 2)
        l_stack = lse[first:first + heads_per_group]

        def one_head(carry, items):
            q_head, o_head, d_head, l_head = items
            scores = jnp.dot(q_head, key_group.T, preferred_element_type=jnp.float32) * factor
            probs = jnp.exp(scores - l_head[:, None])
            probs_low = probs.astype(jnp.bfloat16)
            dv_term = jnp.dot(probs_low.T, d_head, preferred_element_type=jnp.float32)
            dprobs = jnp.dot(d_head, value_group.T, preferred_element_type=jnp.float32)
            delta = jnp.sum(d_head.astype(jnp.float32) * o_head.astype(jnp.float32), axis=1)
            dscores = (probs * (dprobs - delta[:, None])).astype(jnp.bfloat16)
            dq_head = (jnp.dot(dscores, key_group, preferred_element_type=jnp.float32) * factor).astype(jnp.bfloat16)
            dk_term = jnp.dot(dscores.T, q_head, preferred_element_type=jnp.float32)
            return (carry[0] + dk_term, carry[1] + dv_term), dq_head

        zero_filled = jnp.zeros((TOTAL_KEYS, HEAD_SIZE), jnp.float32)
        (dk_sum, dv_sum), dq_stack = lax.scan(one_head, (zero_filled, zero_filled), (q_stack, o_stack, d_stack, l_stack))
        dq_parts.append(dq_stack.transpose(1, 0, 2).reshape(SQ, heads_per_group * HEAD_SIZE))
        dk_parts.append((dk_sum * factor).astype(jnp.bfloat16))
        dv_parts.append(dv_sum.astype(jnp.bfloat16))
    return (jnp.concatenate(dq_parts, axis=1), jnp.concatenate(dk_parts, axis=1), jnp.concatenate(dv_parts, axis=1))
```

```python
import functools

import jax
import jax.numpy as jnp
from jax import lax
from jax.experimental import pallas as pl
from jax.experimental.pallas import tpu as pltpu
from jax.sharding import PartitionSpec as P

KEY_VALUE_HEADS = 4
HEAD_SIZE = 128
FACTOR = HEAD_SIZE ** (-0.5)
NT = (((1,), (1,)), ((), ()))
TN = (((0,), (0,)), ((), ()))
BATCH = 4
VMEM_LIMIT = 60 * 1024 * 1024
FREE = pl.CostEstimate(flops=0, bytes_accessed=0, transcendentals=0)


def split_kernel(dout_ref, *refs):
    out_refs, (block_ref, in_sems, out_sems) = refs[:-3], refs[-3:]
    width = out_refs[0].shape[1]
    columns = BATCH * width
    me = lax.axis_index("head")
    within = lax.rem(me, BATCH)
    reads, writes = [], []
    groups = list(reversed(range(len(out_refs) // BATCH)))
    for group in groups:
        start = pl.multiple_of((me // BATCH ^ group) * columns, columns)
        reads.append(
            pltpu.make_async_copy(
                dout_ref.at[:, pl.ds(start, columns)], block_ref.at[group], in_sems.at[group]
            )
        )
        reads[-1].start()
    for read, group in zip(reads, groups):
        read.wait()
        for index in range(BATCH):
            distance = group * BATCH + index
            start = pl.multiple_of((within ^ index) * width, width)
            writes.append(
                pltpu.make_async_copy(
                    block_ref.at[group, :, pl.ds(start, width)],
                    out_refs[distance],
                    out_sems.at[distance],
                )
            )
            writes[-1].start()
    for write in writes:
        write.wait()


def split(dout, dests):
    rows, width = dout.shape[0], dout.shape[1] // dests
    groups = dests // BATCH
    return pl.pallas_call(
        split_kernel,
        in_specs=[pl.BlockSpec(memory_space=pl.ANY)],
        out_specs=[pl.BlockSpec(memory_space=pl.ANY)] * dests,
        out_shape=[jax.ShapeDtypeStruct((rows, width), dout.dtype)] * dests,
        scratch_shapes=[
            pltpu.VMEM((groups, rows, BATCH * width), dout.dtype),
            pltpu.SemaphoreType.DMA((groups,)),
            pltpu.SemaphoreType.DMA((dests,)),
        ],
        compiler_params=pltpu.CompilerParams(vmem_limit_bytes=VMEM_LIMIT),
        cost_estimate=FREE,
        name="split",
    )(dout)


def attention_kernel(first, last, pieces, place_ref, *refs):
    d_refs = refs[:pieces]
    q_ref, o_ref, lse_ref, k_ref, v_ref = refs[pieces : pieces + 5]
    refs = refs[pieces + 5 :]
    if not first:
        dk_old, dv_old = refs[1:3]
        refs = refs[3:]
    dq_ref = refs[0]
    if last:
        terms_ref, d_ref, dk_ref, dv_ref = refs[1:]
    else:
        dk_ref, dv_ref, d_ref = refs[1:]
    step = pl.program_id(0)

    @pl.when(step == 0)
    def _():
        if first:
            dk_ref[...] = jnp.zeros_like(dk_ref)
            dv_ref[...] = jnp.zeros_like(dv_ref)
        else:
            dk_ref[...] = dk_old[...]
            dv_ref[...] = dv_old[...]
        rows = d_refs[0].shape[0]
        for index in range(pieces):
            start = (lax.rem(place_ref[0], pieces) ^ index) * rows
            d_ref[pl.ds(pl.multiple_of(start, rows), rows), :] = d_refs[index][...]

    block, width = q_ref.shape
    columns = [slice(start, start + HEAD_SIZE) for start in range(0, width, HEAD_SIZE)]

    def stacked(array):
        return jnp.concatenate([array[:, c] for c in columns], axis=0)

    q, o, k, v = stacked(q_ref), stacked(o_ref), k_ref[...], v_ref[...]
    d = stacked(d_ref[pl.ds(pl.multiple_of(step * block, block), block), :])
    lse = jnp.concatenate([lse_ref[h : h + 1, :] for h in range(len(columns))], axis=1)
    scores = lax.dot_general(k, q, NT, preferred_element_type=jnp.float32) * FACTOR
    probs = jnp.exp(scores - lse)
    product = d.astype(jnp.float32) * o.astype(jnp.float32)
    high = product.astype(jnp.bfloat16)
    low = (product - high.astype(jnp.float32)).astype(jnp.bfloat16)
    minus = jnp.full(v.shape, -1.0, jnp.bfloat16)
    dprobs_less_delta = lax.dot_general(
        jnp.concatenate([v, minus, minus], axis=1),
        jnp.concatenate([d, high, low], axis=1),
        NT,
        preferred_element_type=jnp.float32,
    )
    dscores = (probs * dprobs_less_delta).astype(jnp.bfloat16)
    dq = lax.dot_general(dscores, k, TN, preferred_element_type=jnp.float32) * FACTOR
    for h, c in enumerate(columns):
        dq_ref[:, c] = dq[h * block : (h + 1) * block].astype(jnp.bfloat16)
    dk_ref[...] += jnp.dot(dscores, q, preferred_element_type=jnp.float32)
    dv_ref[...] += jnp.dot(probs.astype(jnp.bfloat16), d, preferred_element_type=jnp.float32)

    if last:

        @pl.when(step == pl.num_programs(0) - 1)
        def _():
            owned = terms_ref.shape[1] // 2
            for owner in range(terms_ref.shape[0]):
                rows = slice(owner * owned, (owner + 1) * owned)
                terms_ref[owner, :owned, :] = dk_ref[rows, :]
                terms_ref[owner, owned:, :] = dv_ref[rows, :]


def attention(start, place, arrived, first, owners, data, carried):
    queries, outputs, lse, k, v = data
    pieces = len(arrived)
    rows, width = arrived[0].shape
    heads = width // HEAD_SIZE
    keys = k.shape[0]
    block, steps = 2 * rows, pieces // 2

    def at(i, place):
        return (place[0] ^ start) // pieces * steps + i

    here = pl.BlockSpec((block, width), lambda i, place: (at(i, place), 0))
    whole = pl.BlockSpec((keys, HEAD_SIZE), lambda i, place: (0, 0))
    in_specs = [pl.BlockSpec((rows, width), lambda i, place: (0, 0))] * pieces + [
        here,
        here,
        pl.BlockSpec((heads, block), lambda i, place: (0, at(i, place))),
        whole,
        whole,
    ]
    operands = [place, *arrived, queries, outputs, lse, k, v]
    aliases = {}
    if not first:
        in_specs += [pl.BlockSpec(memory_space=pl.ANY), whole, whole]
        aliases = {len(operands): 0}
        operands += carried
    out_specs = [here]
    out_shape = [jax.ShapeDtypeStruct(queries.shape, jnp.bfloat16)]
    scratch = [pltpu.VMEM((pieces * rows, width), jnp.bfloat16)]
    if owners:
        terms = (owners, 2 * keys // owners, HEAD_SIZE)
        out_specs += [pl.BlockSpec(terms, lambda i, place: (0, 0, 0))]
        out_shape += [jax.ShapeDtypeStruct(terms, jnp.float32)]
        scratch += [pltpu.VMEM((keys, HEAD_SIZE), jnp.float32)] * 2
    else:
        out_specs += [whole, whole]
        out_shape += [jax.ShapeDtypeStruct((keys, HEAD_SIZE), jnp.float32)] * 2
    return pl.pallas_call(
        functools.partial(attention_kernel, first, owners > 0, pieces),
        grid_spec=pltpu.PrefetchScalarGridSpec(
            num_scalar_prefetch=1,
            grid=(steps,),
            in_specs=in_specs,
            out_specs=out_specs,
            scratch_shapes=scratch,
        ),
        out_shape=out_shape,
        input_output_aliases=aliases,
        compiler_params=pltpu.CompilerParams(vmem_limit_bytes=VMEM_LIMIT),
        cost_estimate=FREE,
        name=f"sources_{start}",
    )(*operands)


def sum_kernel(terms_ref, dk_ref, dv_ref):
    groups = KEY_VALUE_HEADS
    senders = terms_ref.shape[0] // groups
    owned = terms_ref.shape[1] // 2
    for group in range(groups):
        total = terms_ref[group * senders]
        for sender in range(1, senders):
            total = total + terms_ref[group * senders + sender]
        columns = slice(group * HEAD_SIZE, (group + 1) * HEAD_SIZE)
        dk_ref[:, columns] = (total[:owned] * FACTOR).astype(jnp.bfloat16)
        dv_ref[:, columns] = total[owned:].astype(jnp.bfloat16)


def swap(array, axis, size, bits):
    return lax.ppermute(array, axis, [(i, i ^ bits) for i in range(size)])


def after(array, *others):
    return lax.optimization_barrier((array,) + others)[0]


def own_group(keys, values, owners):
    owned = keys.shape[0]
    each = owners // KEY_VALUE_HEADS

    def kernel(k_ref, v_ref, out_ref):
        for group in range(KEY_VALUE_HEADS):
            columns = slice(group * HEAD_SIZE, (group + 1) * HEAD_SIZE)
            both = jnp.concatenate(
                [k_ref[:, columns].astype(jnp.float32), v_ref[:, columns].astype(jnp.float32)],
                axis=0,
            ).astype(keys.dtype)
            for index in range(each):
                out_ref[group * each + index] = both

    mine = pl.pallas_call(
        kernel,
        in_specs=[pl.BlockSpec(memory_space=pltpu.VMEM)] * 2,
        out_shape=jax.ShapeDtypeStruct((owners, 2 * owned, HEAD_SIZE), keys.dtype),
        name="pack_keys",
    )(keys, values)
    got = lax.all_to_all(mine, ("head", "ctx"), split_axis=0, concat_axis=0, tiled=True)
    return got[:, :owned].reshape(-1, HEAD_SIZE), got[:, owned:].reshape(-1, HEAD_SIZE)


def on_device(heads_axis, ctx_axis, queries, keys, values, outputs, dout, lse):
    near = heads_axis // 2
    owners = heads_axis * ctx_axis
    place = lax.axis_index("head").astype(jnp.int32).reshape(1)
    k, v = own_group(keys, values, owners)

    pieces = split(dout, heads_axis)
    arrived = {0: pieces[0]}

    def send(distance, *others):
        piece = after(pieces[distance], *others)
        arrived[distance] = swap(piece, "head", heads_axis, distance)

    data = (queries, outputs, lse, k, v)

    def compute(start, count, carried):
        return attention(
            start,
            place,
            [arrived[distance] for distance in range(start, start + count)],
            start == 0,
            owners if start + count == heads_axis else 0,
            data,
            carried,
        )

    for beside in range(1, near):
        send(beside, *([arrived[beside - 3]] if beside > 3 else []))
    held, carried = list(range(0, near, BATCH)), []
    for distance in range(near, heads_axis):
        gates = [arrived[distance - 3]] if distance >= near + 3 else []
        while held and distance >= heads_axis - (3 if not carried else 0):
            carried = compute(held.pop(0), BATCH, carried)
            gates.append(carried[1])
        if 0 and not carried and distance >= near + 0:
            gates.append(arrived[min(distance - near - 0 + 1, near - 1)])
        send(distance, *gates)
    for start in held + list(range(near, heads_axis - BATCH, BATCH)):
        carried = compute(start, BATCH, carried)
    for start in range(heads_axis - BATCH, heads_axis, 2):
        carried = compute(start, 2, carried)
    dq, terms = carried

    terms = lax.all_to_all(terms, ("head", "ctx"), split_axis=0, concat_axis=0, tiled=True)
    shape = jax.ShapeDtypeStruct(keys.shape, jnp.bfloat16)
    small = pltpu.CompilerParams(vmem_limit_bytes=8 * 1024 * 1024)
    dk, dv = pl.pallas_call(
        sum_kernel, out_shape=[shape, shape], compiler_params=small, name="sum_terms"
    )(terms)
    return dq, dk, dv


def solution(mesh):
    placed = (
        P("ctx", "head"),
        P(("head", "ctx"), None),
        P(("head", "ctx"), None),
        P("ctx", "head"),
        P(("ctx", "head"), None),
        P("head", "ctx"),
    )
    return jax.shard_map(
        functools.partial(on_device, mesh.shape["head"], mesh.shape["ctx"]),
        mesh=mesh,
        in_specs=placed,
        out_specs=(P("ctx", "head"), P(("head", "ctx"), None), P(("head", "ctx"), None)),
        check_vma=False,
    )
```

```python
import functools

import jax
import jax.numpy as jnp
from jax import lax
from jax.experimental import pallas as pl
from jax.experimental.pallas import tpu as pltpu
from jax.sharding import PartitionSpec as P

KEY_VALUE_HEADS = 4
HEAD_SIZE = 128
FACTOR = HEAD_SIZE ** (-0.5)
NT = (((1,), (1,)), ((), ()))
TN = (((0,), (0,)), ((), ()))
BATCH = 4
VMEM_LIMIT = 60 * 1024 * 1024
FREE = pl.CostEstimate(flops=0, bytes_accessed=0, transcendentals=0)


def batches(heads_axis):
    near = heads_axis // 2
    found = [(far, heads_axis - BATCH - far) for far in range(near, heads_axis, BATCH)]
    return found + [(odd, even) for even, odd in found]


def by_place(pair, odd):
    return pair[0] + odd * (pair[1] - pair[0])


def sent_distance(bases, index, odd):
    return by_place(bases, odd ^ (index % 2)) + index


def split_kernel(all_bases, dout_ref, *refs):
    out_refs, (block_ref, in_sems, out_sems) = refs[:-3], refs[-3:]
    width = out_refs[0].shape[1]
    columns = BATCH * width
    me = lax.axis_index("head")
    reads = []
    for group in range(block_ref.shape[0]):
        reads.append(
            pltpu.make_async_copy(
                dout_ref.at[:, group * columns : (group + 1) * columns],
                block_ref.at[group],
                in_sems.at[group],
            )
        )
        reads[-1].start()
    for read in reads:
        read.wait()
    writes = []
    for place, out_ref in enumerate(out_refs):
        target = me ^ sent_distance(all_bases[place // BATCH], place % BATCH, lax.rem(me, 2))
        start = pl.multiple_of(lax.rem(target, BATCH) * width, width)
        piece = block_ref.at[target // BATCH, :, pl.ds(start, width)]
        writes.append(pltpu.make_async_copy(piece, out_ref, out_sems.at[place]))
        writes[-1].start()
    for write in writes:
        write.wait()


def split(dout, dests):
    rows, width = dout.shape[0], dout.shape[1] // dests
    groups = dests // BATCH
    return pl.pallas_call(
        functools.partial(split_kernel, batches(dests)),
        in_specs=[pl.BlockSpec(memory_space=pl.ANY)],
        out_specs=[pl.BlockSpec(memory_space=pl.ANY)] * dests,
        out_shape=[jax.ShapeDtypeStruct((rows, width), dout.dtype)] * dests,
        scratch_shapes=[
            pltpu.VMEM((groups, rows, BATCH * width), dout.dtype),
            pltpu.SemaphoreType.DMA((groups,)),
            pltpu.SemaphoreType.DMA((dests,)),
        ],
        compiler_params=pltpu.CompilerParams(vmem_limit_bytes=VMEM_LIMIT),
        cost_estimate=FREE,
        name="split",
    )(dout)


def attention_kernel(first, last, pairs, place_ref, *refs):
    pieces = len(pairs)
    d_refs = refs[:pieces]
    q_ref, o_ref, lse_ref, k_ref, v_ref = refs[pieces : pieces + 5]
    refs = refs[pieces + 5 :]
    if not first:
        dk_old, dv_old = refs[1:3]
        refs = refs[3:]
    dq_ref = refs[0]
    if last:
        terms_ref, d_ref, dk_ref, dv_ref = refs[1:]
    else:
        dk_ref, dv_ref, d_ref = refs[1:]
    step = pl.program_id(0)

    @pl.when(step == 0)
    def _():
        if first:
            dk_ref[...] = jnp.zeros_like(dk_ref)
            dv_ref[...] = jnp.zeros_like(dv_ref)
        else:
            dk_ref[...] = dk_old[...]
            dv_ref[...] = dv_old[...]
        rows = d_refs[0].shape[0]
        for index in range(pieces):
            distance = by_place(pairs[index], lax.rem(place_ref[0], 2))
            start = lax.rem(place_ref[0] ^ distance, pieces) * rows
            d_ref[pl.ds(pl.multiple_of(start, rows), rows), :] = d_refs[index][...]

    block, width = q_ref.shape
    columns = [slice(start, start + HEAD_SIZE) for start in range(0, width, HEAD_SIZE)]

    def stacked(array):
        return jnp.concatenate([array[:, c] for c in columns], axis=0)

    q, o, k, v = stacked(q_ref), stacked(o_ref), k_ref[...], v_ref[...]
    d = stacked(d_ref[pl.ds(pl.multiple_of(step * block, block), block), :])
    lse = jnp.concatenate([lse_ref[h : h + 1, :] for h in range(len(columns))], axis=1)
    scores = lax.dot_general(k, q, NT, preferred_element_type=jnp.float32) * FACTOR
    probs = jnp.exp(scores - lse)
    product = d.astype(jnp.float32) * o.astype(jnp.float32)
    high = product.astype(jnp.bfloat16)
    low = (product - high.astype(jnp.float32)).astype(jnp.bfloat16)
    minus = jnp.full(v.shape, -1.0, jnp.bfloat16)
    dprobs_less_delta = lax.dot_general(
        jnp.concatenate([v, minus, minus], axis=1),
        jnp.concatenate([d, high, low], axis=1),
        NT,
        preferred_element_type=jnp.float32,
    )
    dscores = (probs * dprobs_less_delta).astype(jnp.bfloat16)
    dq = lax.dot_general(dscores, k, TN, preferred_element_type=jnp.float32) * FACTOR
    for h, c in enumerate(columns):
        dq_ref[:, c] = dq[h * block : (h + 1) * block].astype(jnp.bfloat16)
    dk_ref[...] += jnp.dot(dscores, q, preferred_element_type=jnp.float32)
    dv_ref[...] += jnp.dot(probs.astype(jnp.bfloat16), d, preferred_element_type=jnp.float32)

    if last:

        @pl.when(step == pl.num_programs(0) - 1)
        def _():
            owned = terms_ref.shape[1] // 2
            for owner in range(terms_ref.shape[0]):
                rows = slice(owner * owned, (owner + 1) * owned)
                terms_ref[owner, :owned, :] = dk_ref[rows, :]
                terms_ref[owner, owned:, :] = dv_ref[rows, :]


def attention(pairs, place, arrived, first, owners, data, carried):
    queries, outputs, lse, k, v = data
    pieces = len(arrived)
    rows, width = arrived[0].shape
    heads = width // HEAD_SIZE
    keys = k.shape[0]
    block, steps = 2 * rows, pieces // 2

    def at(i, place):
        return (place[0] ^ by_place(pairs[0], lax.rem(place[0], 2))) // pieces * steps + i

    here = pl.BlockSpec((block, width), lambda i, place: (at(i, place), 0))
    whole = pl.BlockSpec((keys, HEAD_SIZE), lambda i, place: (0, 0))
    in_specs = [pl.BlockSpec((rows, width), lambda i, place: (0, 0))] * pieces + [
        here,
        here,
        pl.BlockSpec((heads, block), lambda i, place: (0, at(i, place))),
        whole,
        whole,
    ]
    operands = [place, *arrived, queries, outputs, lse, k, v]
    aliases = {}
    if not first:
        in_specs += [pl.BlockSpec(memory_space=pl.ANY), whole, whole]
        aliases = {len(operands): 0}
        operands += carried
    out_specs = [here]
    out_shape = [jax.ShapeDtypeStruct(queries.shape, jnp.bfloat16)]
    scratch = [pltpu.VMEM((pieces * rows, width), jnp.bfloat16)]
    if owners:
        terms = (owners, 2 * keys // owners, HEAD_SIZE)
        out_specs += [pl.BlockSpec(terms, lambda i, place: (0, 0, 0))]
        out_shape += [jax.ShapeDtypeStruct(terms, jnp.float32)]
        scratch += [pltpu.VMEM((keys, HEAD_SIZE), jnp.float32)] * 2
    else:
        out_specs += [whole, whole]
        out_shape += [jax.ShapeDtypeStruct((keys, HEAD_SIZE), jnp.float32)] * 2
    return pl.pallas_call(
        functools.partial(attention_kernel, first, owners > 0, pairs),
        grid_spec=pltpu.PrefetchScalarGridSpec(
            num_scalar_prefetch=1,
            grid=(steps,),
            in_specs=in_specs,
            out_specs=out_specs,
            scratch_shapes=scratch,
        ),
        out_shape=out_shape,
        input_output_aliases=aliases,
        compiler_params=pltpu.CompilerParams(vmem_limit_bytes=VMEM_LIMIT),
        cost_estimate=FREE,
        name=f"sources_{pairs[0][0]}",
    )(*operands)


def sum_kernel(terms_ref, dk_ref, dv_ref):
    groups = KEY_VALUE_HEADS
    senders = terms_ref.shape[0] // groups
    owned = terms_ref.shape[1] // 2
    for group in range(groups):
        total = terms_ref[group * senders]
        for sender in range(1, senders):
            total = total + terms_ref[group * senders + sender]
        columns = slice(group * HEAD_SIZE, (group + 1) * HEAD_SIZE)
        dk_ref[:, columns] = (total[:owned] * FACTOR).astype(jnp.bfloat16)
        dv_ref[:, columns] = total[owned:].astype(jnp.bfloat16)


def swap(array, axis, size, bits):
    return lax.ppermute(array, axis, [(i, i ^ bits) for i in range(size)])


def after(array, *others):
    return lax.optimization_barrier((array,) + others)[0]


def own_group(keys, values, owners):
    owned = keys.shape[0]
    each = owners // KEY_VALUE_HEADS

    def kernel(k_ref, v_ref, out_ref):
        for group in range(KEY_VALUE_HEADS):
            columns = slice(group * HEAD_SIZE, (group + 1) * HEAD_SIZE)
            both = jnp.concatenate(
                [k_ref[:, columns].astype(jnp.float32), v_ref[:, columns].astype(jnp.float32)],
                axis=0,
            ).astype(keys.dtype)
            for index in range(each):
                out_ref[group * each + index] = both

    mine = pl.pallas_call(
        kernel,
        in_specs=[pl.BlockSpec(memory_space=pltpu.VMEM)] * 2,
        out_shape=jax.ShapeDtypeStruct((owners, 2 * owned, HEAD_SIZE), keys.dtype),
        name="pack_keys",
    )(keys, values)
    got = lax.all_to_all(mine, ("head", "ctx"), split_axis=0, concat_axis=0, tiled=True)
    return got[:, :owned].reshape(-1, HEAD_SIZE), got[:, owned:].reshape(-1, HEAD_SIZE)


def on_device(heads_axis, ctx_axis, queries, keys, values, outputs, dout, lse):
    owners = heads_axis * ctx_axis
    all_bases = batches(heads_axis)
    place = lax.axis_index("head").astype(jnp.int32).reshape(1)
    k, v = own_group(keys, values, owners)
    pieces = split(dout, heads_axis)
    data = (queries, outputs, lse, k, v)
    arrived = []

    def send(*gates):
        batch, index = divmod(len(arrived), BATCH)
        piece = after(pieces[len(arrived)], *gates)
        pairs = [
            (i, i ^ sent_distance(all_bases[batch], index, i % 2)) for i in range(heads_axis)
        ]
        arrived.append(lax.ppermute(piece, "head", pairs))

    def compute(start, count, carried):
        pairs = [
            tuple(base + i % BATCH for base in all_bases[i // BATCH])
            for i in range(start, start + count)
        ]
        return attention(
            pairs,
            place,
            arrived[start : start + count],
            start == 0,
            owners if start + count == heads_axis else 0,
            data,
            carried,
        )

    near = heads_axis // 2
    carried = []
    for place_in_order in range(heads_axis):
        gates = [arrived[place_in_order - 0]] if 0 and place_in_order >= 0 else []
        if 5 and place_in_order == near + 5:
            carried = compute(0, near, carried)
        if 5 and place_in_order >= near + 5:
            gates.append(carried[1])
        send(*gates)
    if not carried:
        carried = compute(0, near, carried)
    for start in range(near, heads_axis, 4):
        carried = compute(start, 4, carried)
    dq, terms = carried

    terms = lax.all_to_all(terms, ("head", "ctx"), split_axis=0, concat_axis=0, tiled=True)
    shape = jax.ShapeDtypeStruct(keys.shape, jnp.bfloat16)
    small = pltpu.CompilerParams(vmem_limit_bytes=8 * 1024 * 1024)
    dk, dv = pl.pallas_call(
        sum_kernel, out_shape=[shape, shape], compiler_params=small, name="sum_terms"
    )(terms)
    return dq, dk, dv


def solution(mesh):
    placed = (
        P("ctx", "head"),
        P(("head", "ctx"), None),
        P(("head", "ctx"), None),
        P("ctx", "head"),
        P(("ctx", "head"), None),
        P("head", "ctx"),
    )
    return jax.shard_map(
        functools.partial(on_device, mesh.shape["head"], mesh.shape["ctx"]),
        mesh=mesh,
        in_specs=placed,
        out_specs=(P("ctx", "head"), P(("head", "ctx"), None), P(("head", "ctx"), None)),
        check_vma=False,
    )
```

```python
import functools

import jax
import jax.numpy as jnp
from jax import lax
from jax.experimental import pallas as pl
from jax.experimental.pallas import tpu as pltpu
from jax.sharding import PartitionSpec as P

KEY_VALUE_HEADS = 4
HEAD_SIZE = 128
FACTOR = HEAD_SIZE ** (-0.5)
NT = (((1,), (1,)), ((), ()))
TN = (((0,), (0,)), ((), ()))
BATCH = 4
VMEM_LIMIT = 60 * 1024 * 1024
SMALL_LIMIT = 24 * 1024 * 1024
FREE = pl.CostEstimate(flops=0, bytes_accessed=0, transcendentals=0)


def batches(heads_axis):
    near = heads_axis // 2
    found = [(far, heads_axis - BATCH - far) for far in range(near, heads_axis, BATCH)]
    return found + [(odd, even) for even, odd in found]


def by_place(pair, odd):
    return pair[0] + odd * (pair[1] - pair[0])


def sent_distance(bases, index, odd):
    return by_place(bases, odd ^ (index % 2)) + index


def split_kernel(all_bases, dout_ref, *refs):
    out_refs, (block_ref, in_sems, out_sems) = refs[:-3], refs[-3:]
    width = out_refs[0].shape[1]
    columns = BATCH * width
    me = lax.axis_index("head")
    mine = me // BATCH
    half = len(all_bases) // 2

    def read(group):
        start = pl.multiple_of((mine ^ group) * columns, columns)
        return pltpu.make_async_copy(
            dout_ref.at[:, pl.ds(start, columns)], block_ref.at[group], in_sems.at[group]
        )

    for pair in all_bases[:half]:
        for base in pair:
            read(base // BATCH).start()
    writes = []
    for batch in range(half):
        for base in all_bases[batch]:
            read(base // BATCH).wait()
        for place in (*range(batch * BATCH, (batch + 1) * BATCH),
                      *range((batch + half) * BATCH, (batch + half + 1) * BATCH)):
            distance = sent_distance(all_bases[place // BATCH], place % BATCH, lax.rem(me, 2))
            start = pl.multiple_of(lax.rem(me ^ distance, BATCH) * width, width)
            piece = block_ref.at[distance // BATCH, :, pl.ds(start, width)]
            writes.append(pltpu.make_async_copy(piece, out_refs[place], out_sems.at[place]))
            writes[-1].start()
    for write in writes:
        write.wait()


def split(dout, dests):
    rows, width = dout.shape[0], dout.shape[1] // dests
    groups = dests // BATCH
    return pl.pallas_call(
        functools.partial(split_kernel, batches(dests)),
        in_specs=[pl.BlockSpec(memory_space=pl.ANY)],
        out_specs=[pl.BlockSpec(memory_space=pl.ANY)] * dests,
        out_shape=[jax.ShapeDtypeStruct((rows, width), dout.dtype)] * dests,
        scratch_shapes=[
            pltpu.VMEM((groups, rows, BATCH * width), dout.dtype),
            pltpu.SemaphoreType.DMA((groups,)),
            pltpu.SemaphoreType.DMA((dests,)),
        ],
        compiler_params=pltpu.CompilerParams(vmem_limit_bytes=VMEM_LIMIT),
        cost_estimate=FREE,
        name="split",
    )(dout)


def attention_kernel(first, last, pairs, place_ref, *refs):
    pieces = len(pairs)
    d_refs = refs[:pieces]
    q_ref, o_ref, lse_ref, k_ref, v_ref = refs[pieces : pieces + 5]
    refs = refs[pieces + 5 :]
    if not first:
        dk_old, dv_old = refs[1:3]
        refs = refs[3:]
    dq_ref = refs[0]
    if last:
        terms_ref, d_ref, dk_ref, dv_ref = refs[1:]
    else:
        dk_ref, dv_ref, d_ref = refs[1:]
    step = pl.program_id(0)

    @pl.when(step == 0)
    def _():
        if first:
            dk_ref[...] = jnp.zeros_like(dk_ref)
            dv_ref[...] = jnp.zeros_like(dv_ref)
        else:
            dk_ref[...] = dk_old[...]
            dv_ref[...] = dv_old[...]
        rows = d_refs[0].shape[0]
        for index in range(pieces):
            distance = by_place(pairs[index], lax.rem(place_ref[0], 2))
            start = lax.rem(place_ref[0] ^ distance, pieces) * rows
            d_ref[pl.ds(pl.multiple_of(start, rows), rows), :] = d_refs[index][...]

    block, width = q_ref.shape
    columns = [slice(start, start + HEAD_SIZE) for start in range(0, width, HEAD_SIZE)]

    def stacked(array):
        return jnp.concatenate([array[:, c] for c in columns], axis=0)

    q, o, k, v = stacked(q_ref), stacked(o_ref), k_ref[...], v_ref[...]
    d = stacked(d_ref[pl.ds(pl.multiple_of(step * block, block), block), :])
    lse = jnp.concatenate([lse_ref[h : h + 1, :] for h in range(len(columns))], axis=1)
    scores = lax.dot_general(k, q, NT, preferred_element_type=jnp.float32) * FACTOR
    probs = jnp.exp(scores - lse)
    product = d.astype(jnp.float32) * o.astype(jnp.float32)
    high = product.astype(jnp.bfloat16)
    low = (product - high.astype(jnp.float32)).astype(jnp.bfloat16)
    minus = jnp.full(v.shape, -1.0, jnp.bfloat16)
    dprobs_less_delta = lax.dot_general(
        jnp.concatenate([v, minus, minus], axis=1),
        jnp.concatenate([d, high, low], axis=1),
        NT,
        preferred_element_type=jnp.float32,
    )
    dscores = (probs * dprobs_less_delta).astype(jnp.bfloat16)
    dq = lax.dot_general(dscores, k, TN, preferred_element_type=jnp.float32) * FACTOR
    for h, c in enumerate(columns):
        dq_ref[:, c] = dq[h * block : (h + 1) * block].astype(jnp.bfloat16)
    dk_ref[...] += jnp.dot(dscores, q, preferred_element_type=jnp.float32)
    dv_ref[...] += jnp.dot(probs.astype(jnp.bfloat16), d, preferred_element_type=jnp.float32)

    if last:

        @pl.when(step == pl.num_programs(0) - 1)
        def _():
            owned = terms_ref.shape[1] // 2
            for owner in range(terms_ref.shape[0]):
                rows = slice(owner * owned, (owner + 1) * owned)
                terms_ref[owner, :owned, :] = dk_ref[rows, :]
                terms_ref[owner, owned:, :] = dv_ref[rows, :]


def attention(pairs, place, arrived, first, owners, data, carried):
    queries, outputs, lse, k, v = data
    pieces = len(arrived)
    rows, width = arrived[0].shape
    heads = width // HEAD_SIZE
    keys = k.shape[0]
    block, steps = 2 * rows, pieces // 2

    def at(i, place):
        return (place[0] ^ by_place(pairs[0], lax.rem(place[0], 2))) // pieces * steps + i

    here = pl.BlockSpec((block, width), lambda i, place: (at(i, place), 0))
    whole = pl.BlockSpec((keys, HEAD_SIZE), lambda i, place: (0, 0))
    in_specs = [pl.BlockSpec((rows, width), lambda i, place: (0, 0))] * pieces + [
        here,
        here,
        pl.BlockSpec((heads, block), lambda i, place: (0, at(i, place))),
        whole,
        whole,
    ]
    operands = [place, *arrived, queries, outputs, lse, k, v]
    aliases = {}
    if not first:
        in_specs += [pl.BlockSpec(memory_space=pl.ANY), whole, whole]
        aliases = {len(operands): 0}
        operands += carried
    out_specs = [here]
    out_shape = [jax.ShapeDtypeStruct(queries.shape, jnp.bfloat16)]
    scratch = [pltpu.VMEM((pieces * rows, width), jnp.bfloat16)]
    if owners:
        terms = (owners, 2 * keys // owners, HEAD_SIZE)
        out_specs += [pl.BlockSpec(terms, lambda i, place: (0, 0, 0))]
        out_shape += [jax.ShapeDtypeStruct(terms, jnp.float32)]
        scratch += [pltpu.VMEM((keys, HEAD_SIZE), jnp.float32)] * 2
    else:
        out_specs += [whole, whole]
        out_shape += [jax.ShapeDtypeStruct((keys, HEAD_SIZE), jnp.float32)] * 2
    return pl.pallas_call(
        functools.partial(attention_kernel, first, owners > 0, pairs),
        grid_spec=pltpu.PrefetchScalarGridSpec(
            num_scalar_prefetch=1,
            grid=(steps,),
            in_specs=in_specs,
            out_specs=out_specs,
            scratch_shapes=scratch,
        ),
        out_shape=out_shape,
        input_output_aliases=aliases,
        compiler_params=pltpu.CompilerParams(
            vmem_limit_bytes=VMEM_LIMIT if first else SMALL_LIMIT
        ),
        cost_estimate=FREE,
        name=f"sources_{pairs[0][0]}",
    )(*operands)


def sum_kernel(terms_ref, dk_ref, dv_ref):
    groups = KEY_VALUE_HEADS
    senders = terms_ref.shape[0] // groups
    owned = terms_ref.shape[1] // 2
    for group in range(groups):
        total = terms_ref[group * senders]
        for sender in range(1, senders):
            total = total + terms_ref[group * senders + sender]
        columns = slice(group * HEAD_SIZE, (group + 1) * HEAD_SIZE)
        dk_ref[:, columns] = (total[:owned] * FACTOR).astype(jnp.bfloat16)
        dv_ref[:, columns] = total[owned:].astype(jnp.bfloat16)


def swap(array, axis, size, bits):
    return lax.ppermute(array, axis, [(i, i ^ bits) for i in range(size)])


def after(array, *others):
    return lax.optimization_barrier((array,) + others)[0]


def own_group(keys, values, owners):
    owned = keys.shape[0]
    each = owners // KEY_VALUE_HEADS

    def kernel(k_ref, v_ref, out_ref):
        for group in range(KEY_VALUE_HEADS):
            columns = slice(group * HEAD_SIZE, (group + 1) * HEAD_SIZE)
            both = jnp.concatenate(
                [k_ref[:, columns].astype(jnp.float32), v_ref[:, columns].astype(jnp.float32)],
                axis=0,
            ).astype(keys.dtype)
            for index in range(each):
                out_ref[group * each + index] = both

    mine = pl.pallas_call(
        kernel,
        in_specs=[pl.BlockSpec(memory_space=pltpu.VMEM)] * 2,
        out_shape=jax.ShapeDtypeStruct((owners, 2 * owned, HEAD_SIZE), keys.dtype),
        name="pack_keys",
    )(keys, values)
    got = lax.all_to_all(mine, ("head", "ctx"), split_axis=0, concat_axis=0, tiled=True)
    return got[:, :owned].reshape(-1, HEAD_SIZE), got[:, owned:].reshape(-1, HEAD_SIZE)


def on_device(heads_axis, ctx_axis, queries, keys, values, outputs, dout, lse):
    owners = heads_axis * ctx_axis
    all_bases = batches(heads_axis)
    place = lax.axis_index("head").astype(jnp.int32).reshape(1)
    k, v = own_group(keys, values, owners)
    pieces = split(dout, heads_axis)
    data = (queries, outputs, lse, k, v)
    arrived = []

    def send(*gates):
        batch, index = divmod(len(arrived), BATCH)
        piece = after(pieces[len(arrived)], *gates)
        pairs = [
            (i, i ^ sent_distance(all_bases[batch], index, i % 2)) for i in range(heads_axis)
        ]
        arrived.append(lax.ppermute(piece, "head", pairs))

    def compute(start, count, carried):
        pairs = [
            tuple(base + i % BATCH for base in all_bases[i // BATCH])
            for i in range(start, start + count)
        ]
        return attention(
            pairs,
            place,
            arrived[start : start + count],
            start == 0,
            owners if start + count == heads_axis else 0,
            data,
            carried,
        )

    near = heads_axis // 2
    carried = []
    for place_in_order in range(heads_axis):
        gates = [arrived[place_in_order - 0]] if 0 and place_in_order >= 0 else []
        if 5 and place_in_order == near + 5:
            carried = compute(0, near, carried)
        if 5 and place_in_order >= near + 5:
            gates.append(carried[1])
        send(*gates)
    if not carried:
        carried = compute(0, near, carried)
    for start in range(near, heads_axis, 4):
        carried = compute(start, 4, carried)
    dq, terms = carried

    terms = lax.all_to_all(terms, ("head", "ctx"), split_axis=0, concat_axis=0, tiled=True)
    shape = jax.ShapeDtypeStruct(keys.shape, jnp.bfloat16)
    small = pltpu.CompilerParams(vmem_limit_bytes=8 * 1024 * 1024)
    dk, dv = pl.pallas_call(
        sum_kernel, out_shape=[shape, shape], compiler_params=small, name="sum_terms"
    )(terms)
    return dq, dk, dv


def solution(mesh):
    placed = (
        P("ctx", "head"),
        P(("head", "ctx"), None),
        P(("head", "ctx"), None),
        P("ctx", "head"),
        P(("ctx", "head"), None),
        P("head", "ctx"),
    )
    return jax.shard_map(
        functools.partial(on_device, mesh.shape["head"], mesh.shape["ctx"]),
        mesh=mesh,
        in_specs=placed,
        out_specs=(P("ctx", "head"), P(("head", "ctx"), None), P(("head", "ctx"), None)),
        check_vma=False,
    )
```

```python
import functools

import jax
import jax.numpy as jnp
from jax import lax
from jax.experimental import pallas as pl
from jax.experimental.pallas import tpu as pltpu
from jax.sharding import PartitionSpec as P

KEY_VALUE_HEADS = 4
HEAD_SIZE = 128
FACTOR = HEAD_SIZE ** (-0.5)
NT = (((1,), (1,)), ((), ()))
TN = (((0,), (0,)), ((), ()))
BATCH = 4
VMEM_LIMIT = 60 * 1024 * 1024
SMALL_LIMIT = 24 * 1024 * 1024
FREE = pl.CostEstimate(flops=0, bytes_accessed=0, transcendentals=0)


def batches(heads_axis):
    near = heads_axis // 2
    found = [(far, heads_axis - BATCH - far) for far in range(near, heads_axis, BATCH)]
    return found + [(odd, even) for even, odd in found]


def by_place(pair, odd):
    return pair[0] + odd * (pair[1] - pair[0])


def sent_distance(bases, index, odd):
    return by_place(bases, odd ^ (index % 2)) + index


def split_kernel(all_bases, places, tokens, dout_ref, *refs):
    out_refs, (block_ref, in_sems, out_sems) = refs[tokens:-3], refs[-3:]
    width = out_refs[0].shape[1]
    columns = BATCH * width
    me = lax.axis_index("head")
    mine = me // BATCH

    def read(group):
        start = pl.multiple_of((mine ^ group) * columns, columns)
        return pltpu.make_async_copy(
            dout_ref.at[:, pl.ds(start, columns)], block_ref.at[group], in_sems.at[group]
        )

    needs = [sorted(base // BATCH for base in all_bases[place // BATCH]) for place in places]
    started, there = [], []
    for need in needs:
        for group in need:
            if group not in started:
                started.append(group)
                read(group).start()
    writes = []
    for place, need, out_ref in zip(places, needs, out_refs):
        for group in need:
            if group not in there:
                there.append(group)
                read(group).wait()
        distance = sent_distance(all_bases[place // BATCH], place % BATCH, lax.rem(me, 2))
        start = pl.multiple_of(lax.rem(me ^ distance, BATCH) * width, width)
        piece = block_ref.at[distance // BATCH, :, pl.ds(start, width)]
        writes.append(pltpu.make_async_copy(piece, out_ref, out_sems.at[len(writes)]))
        writes[-1].start()
    for write in writes:
        write.wait()


def split(dout, dests, places, tokens):
    rows, width = dout.shape[0], dout.shape[1] // dests
    groups = dests // BATCH
    return pl.pallas_call(
        functools.partial(split_kernel, batches(dests), places, len(tokens)),
        in_specs=[pl.BlockSpec(memory_space=pl.ANY)] * (1 + len(tokens)),
        out_specs=[pl.BlockSpec(memory_space=pl.ANY)] * len(places),
        out_shape=[jax.ShapeDtypeStruct((rows, width), dout.dtype)] * len(places),
        scratch_shapes=[
            pltpu.VMEM((groups, rows, BATCH * width), dout.dtype),
            pltpu.SemaphoreType.DMA((groups,)),
            pltpu.SemaphoreType.DMA((len(places),)),
        ],
        compiler_params=pltpu.CompilerParams(vmem_limit_bytes=VMEM_LIMIT),
        cost_estimate=FREE,
        name=f"split_{places[0]}",
    )(dout, *tokens)


def attention_kernel(first, last, pairs, place_ref, *refs):
    pieces = len(pairs)
    d_refs = refs[:pieces]
    q_ref, o_ref, lse_ref, k_ref, v_ref = refs[pieces : pieces + 5]
    refs = refs[pieces + 5 :]
    if not first:
        dk_old, dv_old = refs[1:3]
        refs = refs[3:]
    dq_ref = refs[0]
    if last:
        terms_ref, d_ref, dk_ref, dv_ref = refs[1:]
    else:
        dk_ref, dv_ref, d_ref = refs[1:]
    step = pl.program_id(0)

    @pl.when(step == 0)
    def _():
        if first:
            dk_ref[...] = jnp.zeros_like(dk_ref)
            dv_ref[...] = jnp.zeros_like(dv_ref)
        else:
            dk_ref[...] = dk_old[...]
            dv_ref[...] = dv_old[...]
        rows = d_refs[0].shape[0]
        for index in range(pieces):
            distance = by_place(pairs[index], lax.rem(place_ref[0], 2))
            start = lax.rem(place_ref[0] ^ distance, pieces) * rows
            d_ref[pl.ds(pl.multiple_of(start, rows), rows), :] = d_refs[index][...]

    block, width = q_ref.shape
    columns = [slice(start, start + HEAD_SIZE) for start in range(0, width, HEAD_SIZE)]

    def stacked(array):
        return jnp.concatenate([array[:, c] for c in columns], axis=0)

    q, o, k, v = stacked(q_ref), stacked(o_ref), k_ref[...], v_ref[...]
    d = stacked(d_ref[pl.ds(pl.multiple_of(step * block, block), block), :])
    lse = jnp.concatenate([lse_ref[h : h + 1, :] for h in range(len(columns))], axis=1)
    scores = lax.dot_general(k, q, NT, preferred_element_type=jnp.float32) * FACTOR
    probs = jnp.exp(scores - lse)
    product = d.astype(jnp.float32) * o.astype(jnp.float32)
    high = product.astype(jnp.bfloat16)
    low = (product - high.astype(jnp.float32)).astype(jnp.bfloat16)
    minus = jnp.full(v.shape, -1.0, jnp.bfloat16)
    dprobs_less_delta = lax.dot_general(
        jnp.concatenate([v, minus, minus], axis=1),
        jnp.concatenate([d, high, low], axis=1),
        NT,
        preferred_element_type=jnp.float32,
    )
    dscores = (probs * dprobs_less_delta).astype(jnp.bfloat16)
    dq = lax.dot_general(dscores, k, TN, preferred_element_type=jnp.float32) * FACTOR
    for h, c in enumerate(columns):
        dq_ref[:, c] = dq[h * block : (h + 1) * block].astype(jnp.bfloat16)
    dk_ref[...] += jnp.dot(dscores, q, preferred_element_type=jnp.float32)
    dv_ref[...] += jnp.dot(probs.astype(jnp.bfloat16), d, preferred_element_type=jnp.float32)

    if last:

        @pl.when(step == pl.num_programs(0) - 1)
        def _():
            owned = terms_ref.shape[1] // 2
            for owner in range(terms_ref.shape[0]):
                rows = slice(owner * owned, (owner + 1) * owned)
                terms_ref[owner, :owned, :] = dk_ref[rows, :]
                terms_ref[owner, owned:, :] = dv_ref[rows, :]


def attention(pairs, place, arrived, first, owners, data, carried):
    queries, outputs, lse, k, v = data
    pieces = len(arrived)
    rows, width = arrived[0].shape
    heads = width // HEAD_SIZE
    keys = k.shape[0]
    block, steps = 2 * rows, pieces // 2

    def at(i, place):
        return (place[0] ^ by_place(pairs[0], lax.rem(place[0], 2))) // pieces * steps + i

    here = pl.BlockSpec((block, width), lambda i, place: (at(i, place), 0))
    whole = pl.BlockSpec((keys, HEAD_SIZE), lambda i, place: (0, 0))
    in_specs = [pl.BlockSpec((rows, width), lambda i, place: (0, 0))] * pieces + [
        here,
        here,
        pl.BlockSpec((heads, block), lambda i, place: (0, at(i, place))),
        whole,
        whole,
    ]
    operands = [place, *arrived, queries, outputs, lse, k, v]
    aliases = {}
    if not first:
        in_specs += [pl.BlockSpec(memory_space=pl.ANY), whole, whole]
        aliases = {len(operands): 0}
        operands += carried
    out_specs = [here]
    out_shape = [jax.ShapeDtypeStruct(queries.shape, jnp.bfloat16)]
    scratch = [pltpu.VMEM((pieces * rows, width), jnp.bfloat16)]
    if owners:
        terms = (owners, 2 * keys // owners, HEAD_SIZE)
        out_specs += [pl.BlockSpec(terms, lambda i, place: (0, 0, 0))]
        out_shape += [jax.ShapeDtypeStruct(terms, jnp.float32)]
        scratch += [pltpu.VMEM((keys, HEAD_SIZE), jnp.float32)] * 2
    else:
        out_specs += [whole, whole]
        out_shape += [jax.ShapeDtypeStruct((keys, HEAD_SIZE), jnp.float32)] * 2
    return pl.pallas_call(
        functools.partial(attention_kernel, first, owners > 0, pairs),
        grid_spec=pltpu.PrefetchScalarGridSpec(
            num_scalar_prefetch=1,
            grid=(steps,),
            in_specs=in_specs,
            out_specs=out_specs,
            scratch_shapes=scratch,
        ),
        out_shape=out_shape,
        input_output_aliases=aliases,
        compiler_params=pltpu.CompilerParams(
            vmem_limit_bytes=VMEM_LIMIT if first else SMALL_LIMIT
        ),
        cost_estimate=FREE,
        name=f"sources_{pairs[0][0]}",
    )(*operands)


def sum_kernel(terms_ref, dk_ref, dv_ref):
    groups = KEY_VALUE_HEADS
    senders = terms_ref.shape[0] // groups
    owned = terms_ref.shape[1] // 2
    for group in range(groups):
        total = terms_ref[group * senders]
        for sender in range(1, senders):
            total = total + terms_ref[group * senders + sender]
        columns = slice(group * HEAD_SIZE, (group + 1) * HEAD_SIZE)
        dk_ref[:, columns] = (total[:owned] * FACTOR).astype(jnp.bfloat16)
        dv_ref[:, columns] = total[owned:].astype(jnp.bfloat16)


def swap(array, axis, size, bits):
    return lax.ppermute(array, axis, [(i, i ^ bits) for i in range(size)])


def after(array, *others):
    return lax.optimization_barrier((array,) + others)[0]


def own_group(keys, values, owners):
    owned = keys.shape[0]
    each = owners // KEY_VALUE_HEADS

    def kernel(k_ref, v_ref, out_ref):
        for group in range(KEY_VALUE_HEADS):
            columns = slice(group * HEAD_SIZE, (group + 1) * HEAD_SIZE)
            both = jnp.concatenate(
                [k_ref[:, columns].astype(jnp.float32), v_ref[:, columns].astype(jnp.float32)],
                axis=0,
            ).astype(keys.dtype)
            for index in range(each):
                out_ref[group * each + index] = both

    mine = pl.pallas_call(
        kernel,
        in_specs=[pl.BlockSpec(memory_space=pltpu.VMEM)] * 2,
        out_shape=jax.ShapeDtypeStruct((owners, 2 * owned, HEAD_SIZE), keys.dtype),
        name="pack_keys",
    )(keys, values)
    got = lax.all_to_all(mine, ("head", "ctx"), split_axis=0, concat_axis=0, tiled=True)
    return got[:, :owned].reshape(-1, HEAD_SIZE), got[:, owned:].reshape(-1, HEAD_SIZE)


def on_device(heads_axis, ctx_axis, queries, keys, values, outputs, dout, lse):
    owners = heads_axis * ctx_axis
    all_bases = batches(heads_axis)
    place = lax.axis_index("head").astype(jnp.int32).reshape(1)
    k, v = own_group(keys, values, owners)
    pieces = list(split(dout, heads_axis, list(range(BATCH)), []))
    pieces += split(dout, heads_axis, list(range(BATCH, heads_axis)), pieces[:1])
    data = (queries, outputs, lse, k, v)
    arrived = []

    def send(*gates):
        batch, index = divmod(len(arrived), BATCH)
        piece = after(pieces[len(arrived)], *gates)
        pairs = [
            (i, i ^ sent_distance(all_bases[batch], index, i % 2)) for i in range(heads_axis)
        ]
        arrived.append(lax.ppermute(piece, "head", pairs))

    def compute(start, count, carried):
        pairs = [
            tuple(base + i % BATCH for base in all_bases[i // BATCH])
            for i in range(start, start + count)
        ]
        return attention(
            pairs,
            place,
            arrived[start : start + count],
            start == 0,
            owners if start + count == heads_axis else 0,
            data,
            carried,
        )

    near = heads_axis // 2
    carried = []
    for place_in_order in range(heads_axis):
        gates = [arrived[place_in_order - 0]] if 0 and place_in_order >= 0 else []
        if 5 and place_in_order == near + 5:
            carried = compute(0, near, carried)
        if 5 and place_in_order >= near + 5:
            gates.append(carried[1])
        send(*gates)
    if not carried:
        carried = compute(0, near, carried)
    for start in range(near, heads_axis, 4):
        carried = compute(start, 4, carried)
    dq, terms = carried

    terms = lax.all_to_all(terms, ("head", "ctx"), split_axis=0, concat_axis=0, tiled=True)
    shape = jax.ShapeDtypeStruct(keys.shape, jnp.bfloat16)
    small = pltpu.CompilerParams(vmem_limit_bytes=8 * 1024 * 1024)
    dk, dv = pl.pallas_call(
        sum_kernel, out_shape=[shape, shape], compiler_params=small, name="sum_terms"
    )(terms)
    return dq, dk, dv


def solution(mesh):
    placed = (
        P("ctx", "head"),
        P(("head", "ctx"), None),
        P(("head", "ctx"), None),
        P("ctx", "head"),
        P(("ctx", "head"), None),
        P("head", "ctx"),
    )
    return jax.shard_map(
        functools.partial(on_device, mesh.shape["head"], mesh.shape["ctx"]),
        mesh=mesh,
        in_specs=placed,
        out_specs=(P("ctx", "head"), P(("head", "ctx"), None), P(("head", "ctx"), None)),
        check_vma=False,
    )
```

```python
import functools

import jax
import jax.numpy as jnp
from jax import lax
from jax.experimental import pallas as pl
from jax.experimental.pallas import tpu as pltpu
from jax.sharding import PartitionSpec as P

KEY_VALUE_HEADS = 4
HEAD_SIZE = 128
FACTOR = HEAD_SIZE ** (-0.5)
NT = (((1,), (1,)), ((), ()))
TN = (((0,), (0,)), ((), ()))
BATCH = 4
VMEM_LIMIT = 60 * 1024 * 1024
SMALL_LIMIT = 24 * 1024 * 1024
FREE = pl.CostEstimate(flops=0, bytes_accessed=0, transcendentals=0)


def batches(heads_axis):
    near = heads_axis // 2
    found = [(far, heads_axis - BATCH - far) for far in range(near, heads_axis, BATCH)]
    return found + [(odd, even) for even, odd in found]


def by_place(pair, odd):
    return pair[0] + odd * (pair[1] - pair[0])


def sent_distance(bases, index, odd):
    return by_place(bases, odd ^ (index % 2)) + index


def split_kernel(all_bases, dout_ref, *refs):
    out_refs, (block_ref, in_sems, out_sems) = refs[:-3], refs[-3:]
    width = out_refs[0].shape[1]
    columns = BATCH * width
    me = lax.axis_index("head")
    mine = me // BATCH
    half = len(all_bases) // 2

    def read(group):
        start = pl.multiple_of((mine ^ group) * columns, columns)
        return pltpu.make_async_copy(
            dout_ref.at[:, pl.ds(start, columns)], block_ref.at[group], in_sems.at[group]
        )

    for pair in all_bases[:half]:
        for base in pair:
            read(base // BATCH).start()
    writes = []
    for batch in range(half):
        for base in all_bases[batch]:
            read(base // BATCH).wait()
        for place in (*range(batch * BATCH, (batch + 1) * BATCH),
                      *range((batch + half) * BATCH, (batch + half + 1) * BATCH)):
            distance = sent_distance(all_bases[place // BATCH], place % BATCH, lax.rem(me, 2))
            start = pl.multiple_of(lax.rem(me ^ distance, BATCH) * width, width)
            piece = block_ref.at[distance // BATCH, :, pl.ds(start, width)]
            writes.append(pltpu.make_async_copy(piece, out_refs[place], out_sems.at[place]))
            writes[-1].start()
    for write in writes:
        write.wait()


def split(dout, dests):
    rows, width = dout.shape[0], dout.shape[1] // dests
    groups = dests // BATCH
    return pl.pallas_call(
        functools.partial(split_kernel, batches(dests)),
        in_specs=[pl.BlockSpec(memory_space=pl.ANY)],
        out_specs=[pl.BlockSpec(memory_space=pl.ANY)] * dests,
        out_shape=[jax.ShapeDtypeStruct((rows, width), dout.dtype)] * dests,
        scratch_shapes=[
            pltpu.VMEM((groups, rows, BATCH * width), dout.dtype),
            pltpu.SemaphoreType.DMA((groups,)),
            pltpu.SemaphoreType.DMA((dests,)),
        ],
        compiler_params=pltpu.CompilerParams(vmem_limit_bytes=VMEM_LIMIT),
        cost_estimate=FREE,
        name="split",
    )(dout)


def attention_kernel(first, last, pairs, place_ref, *refs):
    pieces = len(pairs)
    d_refs = refs[:pieces]
    q_ref, o_ref, lse_ref, k_ref, v_ref = refs[pieces : pieces + 5]
    refs = refs[pieces + 5 :]
    if not first:
        dk_old, dv_old = refs[1:3]
        refs = refs[3:]
    dq_ref = refs[0]
    if last:
        terms_ref, d_ref, dk_ref, dv_ref = refs[1:]
    else:
        dk_ref, dv_ref, d_ref = refs[1:]
    step = pl.program_id(0)

    @pl.when(step == 0)
    def _():
        if first:
            dk_ref[...] = jnp.zeros_like(dk_ref)
            dv_ref[...] = jnp.zeros_like(dv_ref)
        else:
            dk_ref[...] = dk_old[...]
            dv_ref[...] = dv_old[...]
        rows = d_refs[0].shape[0]
        for index in range(pieces):
            distance = by_place(pairs[index], lax.rem(place_ref[0], 2))
            start = lax.rem(place_ref[0] ^ distance, pieces) * rows
            d_ref[pl.ds(pl.multiple_of(start, rows), rows), :] = d_refs[index][...]

    block, width = q_ref.shape
    columns = [slice(start, start + HEAD_SIZE) for start in range(0, width, HEAD_SIZE)]

    def stacked(array):
        return jnp.concatenate([array[:, c] for c in columns], axis=0)

    q, o, k, v = stacked(q_ref), stacked(o_ref), k_ref[...], v_ref[...]
    d = stacked(d_ref[pl.ds(pl.multiple_of(step * block, block), block), :])
    lse = jnp.concatenate([lse_ref[h : h + 1, :] for h in range(len(columns))], axis=1)
    scores = lax.dot_general(k, q, NT, preferred_element_type=jnp.float32) * FACTOR
    probs = jnp.exp(scores - lse)
    product = d.astype(jnp.float32) * o.astype(jnp.float32)
    high = product.astype(jnp.bfloat16)
    low = (product - high.astype(jnp.float32)).astype(jnp.bfloat16)
    minus = jnp.full(v.shape, -1.0, jnp.bfloat16)
    dprobs_less_delta = lax.dot_general(
        jnp.concatenate([v, minus, minus], axis=1),
        jnp.concatenate([d, high, low], axis=1),
        NT,
        preferred_element_type=jnp.float32,
    )
    dscores = (probs * dprobs_less_delta).astype(jnp.bfloat16)
    dq = lax.dot_general(dscores, k, TN, preferred_element_type=jnp.float32) * FACTOR
    for h, c in enumerate(columns):
        dq_ref[:, c] = dq[h * block : (h + 1) * block].astype(jnp.bfloat16)
    dk_ref[...] += jnp.dot(dscores, q, preferred_element_type=jnp.float32)
    dv_ref[...] += jnp.dot(probs.astype(jnp.bfloat16), d, preferred_element_type=jnp.float32)

    if last:

        @pl.when(step == pl.num_programs(0) - 1)
        def _():
            owned = terms_ref.shape[1] // 2
            for owner in range(terms_ref.shape[0]):
                rows = slice(owner * owned, (owner + 1) * owned)
                terms_ref[owner, :owned, :] = dk_ref[rows, :]
                terms_ref[owner, owned:, :] = dv_ref[rows, :]


def attention(pairs, place, arrived, first, owners, data, carried):
    queries, outputs, lse, k, v = data
    pieces = len(arrived)
    rows, width = arrived[0].shape
    heads = width // HEAD_SIZE
    keys = k.shape[0]
    block, steps = 2 * rows, pieces // 2

    def at(i, place):
        return (place[0] ^ by_place(pairs[0], lax.rem(place[0], 2))) // pieces * steps + i

    here = pl.BlockSpec((block, width), lambda i, place: (at(i, place), 0))
    whole = pl.BlockSpec((keys, HEAD_SIZE), lambda i, place: (0, 0))
    in_specs = [pl.BlockSpec((rows, width), lambda i, place: (0, 0))] * pieces + [
        here,
        here,
        pl.BlockSpec((heads, block), lambda i, place: (0, at(i, place))),
        whole,
        whole,
    ]
    operands = [place, *arrived, queries, outputs, lse, k, v]
    aliases = {}
    if not first:
        in_specs += [pl.BlockSpec(memory_space=pl.ANY), whole, whole]
        aliases = {len(operands): 0}
        operands += carried
    out_specs = [here]
    out_shape = [jax.ShapeDtypeStruct(queries.shape, jnp.bfloat16)]
    scratch = [pltpu.VMEM((pieces * rows, width), jnp.bfloat16)]
    if owners:
        terms = (owners, 2 * keys // owners, HEAD_SIZE)
        out_specs += [pl.BlockSpec(terms, lambda i, place: (0, 0, 0))]
        out_shape += [jax.ShapeDtypeStruct(terms, jnp.float32)]
        scratch += [pltpu.VMEM((keys, HEAD_SIZE), jnp.float32)] * 2
    else:
        out_specs += [whole, whole]
        out_shape += [jax.ShapeDtypeStruct((keys, HEAD_SIZE), jnp.float32)] * 2
    return pl.pallas_call(
        functools.partial(attention_kernel, first, owners > 0, pairs),
        grid_spec=pltpu.PrefetchScalarGridSpec(
            num_scalar_prefetch=1,
            grid=(steps,),
            in_specs=in_specs,
            out_specs=out_specs,
            scratch_shapes=scratch,
        ),
        out_shape=out_shape,
        input_output_aliases=aliases,
        compiler_params=pltpu.CompilerParams(
            vmem_limit_bytes=VMEM_LIMIT if first else SMALL_LIMIT
        ),
        cost_estimate=FREE,
        name=f"sources_{pairs[0][0]}",
    )(*operands)


def sum_kernel(terms_ref, dk_ref, dv_ref):
    groups = KEY_VALUE_HEADS
    senders = terms_ref.shape[0] // groups
    owned = terms_ref.shape[1] // 2
    for group in range(groups):
        total = terms_ref[group * senders]
        for sender in range(1, senders):
            total = total + terms_ref[group * senders + sender]
        columns = slice(group * HEAD_SIZE, (group + 1) * HEAD_SIZE)
        dk_ref[:, columns] = (total[:owned] * FACTOR).astype(jnp.bfloat16)
        dv_ref[:, columns] = total[owned:].astype(jnp.bfloat16)


def swap(array, axis, size, bits):
    return lax.ppermute(array, axis, [(i, i ^ bits) for i in range(size)])


def after(array, *others):
    return lax.optimization_barrier((array,) + others)[0]


def own_group(keys, values, owners):
    owned = keys.shape[0]
    each = owners // KEY_VALUE_HEADS

    def kernel(k_ref, v_ref, out_ref):
        for group in range(KEY_VALUE_HEADS):
            columns = slice(group * HEAD_SIZE, (group + 1) * HEAD_SIZE)
            both = jnp.concatenate(
                [k_ref[:, columns].astype(jnp.float32), v_ref[:, columns].astype(jnp.float32)],
                axis=0,
            ).astype(keys.dtype)
            for index in range(each):
                out_ref[group * each + index] = both

    mine = pl.pallas_call(
        kernel,
        in_specs=[pl.BlockSpec(memory_space=pltpu.VMEM)] * 2,
        out_shape=jax.ShapeDtypeStruct((owners, 2 * owned, HEAD_SIZE), keys.dtype),
        name="pack_keys",
    )(keys, values)
    got = lax.all_to_all(mine, ("head", "ctx"), split_axis=0, concat_axis=0, tiled=True)
    return got[:, :owned].reshape(-1, HEAD_SIZE), got[:, owned:].reshape(-1, HEAD_SIZE)


def on_device(heads_axis, ctx_axis, queries, keys, values, outputs, dout, lse):
    owners = heads_axis * ctx_axis
    all_bases = batches(heads_axis)
    place = lax.axis_index("head").astype(jnp.int32).reshape(1)
    k, v = own_group(keys, values, owners)
    pieces = split(dout, heads_axis)
    data = (queries, outputs, lse, k, v)
    arrived = []

    def send(*gates):
        batch, index = divmod(len(arrived), BATCH)
        piece = after(pieces[len(arrived)], *gates)
        pairs = [
            (i, i ^ sent_distance(all_bases[batch], index, i % 2)) for i in range(heads_axis)
        ]
        arrived.append(lax.ppermute(piece, "head", pairs))

    def compute(start, count, carried):
        pairs = [
            tuple(base + i % BATCH for base in all_bases[i // BATCH])
            for i in range(start, start + count)
        ]
        return attention(
            pairs,
            place,
            arrived[start : start + count],
            start == 0,
            owners if start + count == heads_axis else 0,
            data,
            carried,
        )

    near = heads_axis // 2
    for place_in_order in range(heads_axis):
        gates = [arrived[place_in_order - 6]] if 6 and place_in_order >= 6 else []
        if place_in_order >= near + 4:
            gates.append(k)
        send(*gates)
    carried = compute(0, near, [])
    for start in range(near, heads_axis, BATCH):
        carried = compute(start, BATCH, carried)
    dq, terms = carried

    terms = lax.all_to_all(terms, ("head", "ctx"), split_axis=0, concat_axis=0, tiled=True)
    shape = jax.ShapeDtypeStruct(keys.shape, jnp.bfloat16)
    small = pltpu.CompilerParams(vmem_limit_bytes=8 * 1024 * 1024)
    dk, dv = pl.pallas_call(
        sum_kernel, out_shape=[shape, shape], compiler_params=small, name="sum_terms"
    )(terms)
    return dq, dk, dv


def solution(mesh):
    placed = (
        P("ctx", "head"),
        P(("head", "ctx"), None),
        P(("head", "ctx"), None),
        P("ctx", "head"),
        P(("ctx", "head"), None),
        P("head", "ctx"),
    )
    return jax.shard_map(
        functools.partial(on_device, mesh.shape["head"], mesh.shape["ctx"]),
        mesh=mesh,
        in_specs=placed,
        out_specs=(P("ctx", "head"), P(("head", "ctx"), None), P(("head", "ctx"), None)),
        check_vma=False,
    )
```

```python
import functools

import jax
import jax.numpy as jnp
from jax import lax
from jax.experimental import pallas as pl
from jax.experimental.pallas import tpu as pltpu
from jax.sharding import PartitionSpec as P

KEY_VALUE_HEADS = 4
HEAD_SIZE = 128
FACTOR = HEAD_SIZE ** (-0.5)
NT = (((1,), (1,)), ((), ()))
TN = (((0,), (0,)), ((), ()))
BATCH = 4
VMEM_LIMIT = 60 * 1024 * 1024
SMALL_LIMIT = 24 * 1024 * 1024
FREE = pl.CostEstimate(flops=0, bytes_accessed=0, transcendentals=0)


def batches(heads_axis):
    near = heads_axis // 2
    found = [(far, heads_axis - BATCH - far) for far in range(near, heads_axis, BATCH)]
    return found + [(odd, even) for even, odd in found]


def by_place(pair, odd):
    return pair[0] + odd * (pair[1] - pair[0])


def sent_distance(bases, index, odd):
    return by_place(bases, odd ^ (index % 2)) + index


def split_kernel(all_bases, dout_ref, *refs):
    out_refs, (block_ref, in_sems, out_sems) = refs[:-3], refs[-3:]
    width = out_refs[0].shape[1]
    columns = BATCH * width
    me = lax.axis_index("head")
    mine = me // BATCH
    half = len(all_bases) // 2

    def read(group):
        start = pl.multiple_of((mine ^ group) * columns, columns)
        return pltpu.make_async_copy(
            dout_ref.at[:, pl.ds(start, columns)], block_ref.at[group], in_sems.at[group]
        )

    for pair in all_bases[:half]:
        for base in pair:
            read(base // BATCH).start()
    writes = []
    for batch in range(half):
        for base in all_bases[batch]:
            read(base // BATCH).wait()
        for place in (*range(batch * BATCH, (batch + 1) * BATCH),
                      *range((batch + half) * BATCH, (batch + half + 1) * BATCH)):
            distance = sent_distance(all_bases[place // BATCH], place % BATCH, lax.rem(me, 2))
            start = pl.multiple_of(lax.rem(me ^ distance, BATCH) * width, width)
            piece = block_ref.at[distance // BATCH, :, pl.ds(start, width)]
            writes.append(pltpu.make_async_copy(piece, out_refs[place], out_sems.at[place]))
            writes[-1].start()
    for write in writes:
        write.wait()


def split(dout, dests):
    rows, width = dout.shape[0], dout.shape[1] // dests
    groups = dests // BATCH
    return pl.pallas_call(
        functools.partial(split_kernel, batches(dests)),
        in_specs=[pl.BlockSpec(memory_space=pl.ANY)],
        out_specs=[pl.BlockSpec(memory_space=pl.ANY)] * dests,
        out_shape=[jax.ShapeDtypeStruct((rows, width), dout.dtype)] * dests,
        scratch_shapes=[
            pltpu.VMEM((groups, rows, BATCH * width), dout.dtype),
            pltpu.SemaphoreType.DMA((groups,)),
            pltpu.SemaphoreType.DMA((dests,)),
        ],
        compiler_params=pltpu.CompilerParams(vmem_limit_bytes=VMEM_LIMIT),
        cost_estimate=FREE,
        name="split",
    )(dout)


def attention_kernel(first, last, pairs, place_ref, *refs):
    pieces = len(pairs)
    d_refs = refs[:pieces]
    q_ref, o_ref, lse_ref, k_ref, v_ref = refs[pieces : pieces + 5]
    refs = refs[pieces + 5 :]
    if not first:
        dk_old, dv_old = refs[1:3]
        refs = refs[3:]
    dq_ref = refs[0]
    if last:
        terms_ref, d_ref, dk_ref, dv_ref = refs[1:]
    else:
        dk_ref, dv_ref, d_ref = refs[1:]
    step = pl.program_id(0)

    @pl.when(step == 0)
    def _():
        if first:
            dk_ref[...] = jnp.zeros_like(dk_ref)
            dv_ref[...] = jnp.zeros_like(dv_ref)
        else:
            dk_ref[...] = dk_old[...]
            dv_ref[...] = dv_old[...]
        rows = d_refs[0].shape[0]
        for index in range(pieces):
            distance = by_place(pairs[index], lax.rem(place_ref[0], 2))
            start = lax.rem(place_ref[0] ^ distance, pieces) * rows
            d_ref[pl.ds(pl.multiple_of(start, rows), rows), :] = d_refs[index][...]

    block, width = q_ref.shape
    columns = [slice(start, start + HEAD_SIZE) for start in range(0, width, HEAD_SIZE)]

    def stacked(array):
        return jnp.concatenate([array[:, c] for c in columns], axis=0)

    q, o, k, v = stacked(q_ref), stacked(o_ref), k_ref[...], v_ref[...]
    d = stacked(d_ref[pl.ds(pl.multiple_of(step * block, block), block), :])
    lse = jnp.concatenate([lse_ref[h : h + 1, :] for h in range(len(columns))], axis=1)
    scores = lax.dot_general(k, q, NT, preferred_element_type=jnp.float32) * FACTOR
    probs = jnp.exp(scores - lse)
    product = d.astype(jnp.float32) * o.astype(jnp.float32)
    high = product.astype(jnp.bfloat16)
    low = (product - high.astype(jnp.float32)).astype(jnp.bfloat16)
    minus = jnp.full(v.shape, -1.0, jnp.bfloat16)
    dprobs_less_delta = lax.dot_general(
        jnp.concatenate([v, minus, minus], axis=1),
        jnp.concatenate([d, high, low], axis=1),
        NT,
        preferred_element_type=jnp.float32,
    )
    dscores = (probs * dprobs_less_delta).astype(jnp.bfloat16)
    dq = lax.dot_general(dscores, k, TN, preferred_element_type=jnp.float32) * FACTOR
    for h, c in enumerate(columns):
        dq_ref[:, c] = dq[h * block : (h + 1) * block].astype(jnp.bfloat16)
    dk_ref[...] += jnp.dot(dscores, q, preferred_element_type=jnp.float32)
    dv_ref[...] += jnp.dot(probs.astype(jnp.bfloat16), d, preferred_element_type=jnp.float32)

    if last:

        @pl.when(step == pl.num_programs(0) - 1)
        def _():
            owned = terms_ref.shape[1] // 2
            for owner in range(terms_ref.shape[0]):
                rows = slice(owner * owned, (owner + 1) * owned)
                terms_ref[owner, :owned, :] = dk_ref[rows, :]
                terms_ref[owner, owned:, :] = dv_ref[rows, :]


def attention(pairs, place, arrived, first, owners, data, carried):
    queries, outputs, lse, k, v = data
    pieces = len(arrived)
    rows, width = arrived[0].shape
    heads = width // HEAD_SIZE
    keys = k.shape[0]
    block, steps = 2 * rows, pieces // 2

    def at(i, place):
        return (place[0] ^ by_place(pairs[0], lax.rem(place[0], 2))) // pieces * steps + i

    here = pl.BlockSpec((block, width), lambda i, place: (at(i, place), 0))
    whole = pl.BlockSpec((keys, HEAD_SIZE), lambda i, place: (0, 0))
    in_specs = [pl.BlockSpec((rows, width), lambda i, place: (0, 0))] * pieces + [
        here,
        here,
        pl.BlockSpec((heads, block), lambda i, place: (0, at(i, place))),
        whole,
        whole,
    ]
    operands = [place, *arrived, queries, outputs, lse, k, v]
    aliases = {}
    if not first:
        in_specs += [pl.BlockSpec(memory_space=pl.ANY), whole, whole]
        aliases = {len(operands): 0}
        operands += carried
    out_specs = [here]
    out_shape = [jax.ShapeDtypeStruct(queries.shape, jnp.bfloat16)]
    scratch = [pltpu.VMEM((pieces * rows, width), jnp.bfloat16)]
    if owners:
        terms = (owners, 2 * keys // owners, HEAD_SIZE)
        out_specs += [pl.BlockSpec(terms, lambda i, place: (0, 0, 0))]
        out_shape += [jax.ShapeDtypeStruct(terms, jnp.float32)]
        scratch += [pltpu.VMEM((keys, HEAD_SIZE), jnp.float32)] * 2
    else:
        out_specs += [whole, whole]
        out_shape += [jax.ShapeDtypeStruct((keys, HEAD_SIZE), jnp.float32)] * 2
    return pl.pallas_call(
        functools.partial(attention_kernel, first, owners > 0, pairs),
        grid_spec=pltpu.PrefetchScalarGridSpec(
            num_scalar_prefetch=1,
            grid=(steps,),
            in_specs=in_specs,
            out_specs=out_specs,
            scratch_shapes=scratch,
        ),
        out_shape=out_shape,
        input_output_aliases=aliases,
        compiler_params=pltpu.CompilerParams(
            vmem_limit_bytes=VMEM_LIMIT if first else SMALL_LIMIT
        ),
        cost_estimate=FREE,
        name=f"sources_{pairs[0][0]}",
    )(*operands)


def sum_kernel(terms_ref, dk_ref, dv_ref):
    groups = KEY_VALUE_HEADS
    senders = terms_ref.shape[0] // groups
    owned = terms_ref.shape[1] // 2
    for group in range(groups):
        total = terms_ref[group * senders]
        for sender in range(1, senders):
            total = total + terms_ref[group * senders + sender]
        columns = slice(group * HEAD_SIZE, (group + 1) * HEAD_SIZE)
        dk_ref[:, columns] = (total[:owned] * FACTOR).astype(jnp.bfloat16)
        dv_ref[:, columns] = total[owned:].astype(jnp.bfloat16)


def swap(array, axis, size, bits):
    return lax.ppermute(array, axis, [(i, i ^ bits) for i in range(size)])


def after(array, *others):
    return lax.optimization_barrier((array,) + others)[0]


def own_group(keys, values, owners):
    owned = keys.shape[0]
    each = owners // KEY_VALUE_HEADS

    def kernel(k_ref, v_ref, out_ref):
        for group in range(KEY_VALUE_HEADS):
            columns = slice(group * HEAD_SIZE, (group + 1) * HEAD_SIZE)
            both = jnp.concatenate(
                [k_ref[:, columns].astype(jnp.float32), v_ref[:, columns].astype(jnp.float32)],
                axis=0,
            ).astype(keys.dtype)
            for index in range(each):
                out_ref[group * each + index] = both

    mine = pl.pallas_call(
        kernel,
        in_specs=[pl.BlockSpec(memory_space=pltpu.VMEM)] * 2,
        out_shape=jax.ShapeDtypeStruct((owners, 2 * owned, HEAD_SIZE), keys.dtype),
        name="pack_keys",
    )(keys, values)
    got = lax.all_to_all(mine, ("head", "ctx"), split_axis=0, concat_axis=0, tiled=True)
    return got[:, :owned].reshape(-1, HEAD_SIZE), got[:, owned:].reshape(-1, HEAD_SIZE)


def on_device(heads_axis, ctx_axis, queries, keys, values, outputs, dout, lse):
    owners = heads_axis * ctx_axis
    all_bases = batches(heads_axis)
    place = lax.axis_index("head").astype(jnp.int32).reshape(1)
    k, v = own_group(keys, values, owners)
    pieces = split(dout, heads_axis)
    data = (queries, outputs, lse, k, v)
    arrived = []

    def send(*gates):
        batch, index = divmod(len(arrived), BATCH)
        piece = after(pieces[len(arrived)], *gates)
        pairs = [
            (i, i ^ sent_distance(all_bases[batch], index, i % 2)) for i in range(heads_axis)
        ]
        arrived.append(lax.ppermute(piece, "head", pairs))

    def compute(start, count, carried):
        pairs = [
            tuple(base + i % BATCH for base in all_bases[i // BATCH])
            for i in range(start, start + count)
        ]
        return attention(
            pairs,
            place,
            arrived[start : start + count],
            start == 0,
            owners if start + count == heads_axis else 0,
            data,
            carried,
        )

    half, carried = heads_axis // 2, []
    for place_in_order in range(heads_axis):
        gates = [arrived[place_in_order - 0]] if 0 and place_in_order >= 0 else []
        if place_in_order == half + 5:
            carried = compute(0, half // 2, carried)
        if place_in_order == half + 6:
            carried = compute(half // 2, half // 2, carried)
        if carried:
            gates.append(carried[1])
        send(*gates)
    for start in range(half, heads_axis, BATCH):
        carried = compute(start, BATCH, carried)
    dq, terms = carried

    terms = lax.all_to_all(terms, ("head", "ctx"), split_axis=0, concat_axis=0, tiled=True)
    shape = jax.ShapeDtypeStruct(keys.shape, jnp.bfloat16)
    small = pltpu.CompilerParams(vmem_limit_bytes=8 * 1024 * 1024)
    dk, dv = pl.pallas_call(
        sum_kernel, out_shape=[shape, shape], compiler_params=small, name="sum_terms"
    )(terms)
    return dq, dk, dv


def solution(mesh):
    placed = (
        P("ctx", "head"),
        P(("head", "ctx"), None),
        P(("head", "ctx"), None),
        P("ctx", "head"),
        P(("ctx", "head"), None),
        P("head", "ctx"),
    )
    return jax.shard_map(
        functools.partial(on_device, mesh.shape["head"], mesh.shape["ctx"]),
        mesh=mesh,
        in_specs=placed,
        out_specs=(P("ctx", "head"), P(("head", "ctx"), None), P(("head", "ctx"), None)),
        check_vma=False,
    )
```

```python
import functools

import jax
import jax.numpy as jnp
from jax import lax
from jax.experimental import pallas as pl
from jax.experimental.pallas import tpu as pltpu
from jax.sharding import PartitionSpec as P

KEY_VALUE_HEADS = 4
HEAD_SIZE = 128
FACTOR = HEAD_SIZE ** (-0.5)
NT = (((1,), (1,)), ((), ()))
TN = (((0,), (0,)), ((), ()))
BATCH = 4
VMEM_LIMIT = 60 * 1024 * 1024
SMALL_LIMIT = 24 * 1024 * 1024
FREE = pl.CostEstimate(flops=0, bytes_accessed=0, transcendentals=0)


def batches(heads_axis):
    near = heads_axis // 2
    found = [(far, heads_axis - BATCH - far) for far in range(near, heads_axis, BATCH)]
    return found + [(odd, even) for even, odd in found]


def by_place(pair, odd):
    return pair[0] + odd * (pair[1] - pair[0])


def sent_distance(bases, index, odd):
    return by_place(bases, odd ^ (index % 2)) + index


def split_kernel(all_bases, dout_ref, *refs):
    out_refs, (block_ref, in_sems, out_sems) = refs[:-3], refs[-3:]
    width = out_refs[0].shape[1]
    columns = BATCH * width
    me = lax.axis_index("head")
    mine = me // BATCH
    half = len(all_bases) // 2

    def read(group):
        start = pl.multiple_of((mine ^ group) * columns, columns)
        return pltpu.make_async_copy(
            dout_ref.at[:, pl.ds(start, columns)], block_ref.at[group], in_sems.at[group]
        )

    for pair in all_bases[:half]:
        for base in pair:
            read(base // BATCH).start()
    writes = []
    for batch in range(half):
        for base in all_bases[batch]:
            read(base // BATCH).wait()
        for place in (*range(batch * BATCH, (batch + 1) * BATCH),
                      *range((batch + half) * BATCH, (batch + half + 1) * BATCH)):
            distance = sent_distance(all_bases[place // BATCH], place % BATCH, lax.rem(me, 2))
            start = pl.multiple_of(lax.rem(me ^ distance, BATCH) * width, width)
            piece = block_ref.at[distance // BATCH, :, pl.ds(start, width)]
            writes.append(pltpu.make_async_copy(piece, out_refs[place], out_sems.at[place]))
            writes[-1].start()
    for write in writes:
        write.wait()


def split(dout, dests):
    rows, width = dout.shape[0], dout.shape[1] // dests
    groups = dests // BATCH
    return pl.pallas_call(
        functools.partial(split_kernel, batches(dests)),
        in_specs=[pl.BlockSpec(memory_space=pl.ANY)],
        out_specs=[pl.BlockSpec(memory_space=pl.ANY)] * dests,
        out_shape=[jax.ShapeDtypeStruct((rows, width), dout.dtype)] * dests,
        scratch_shapes=[
            pltpu.VMEM((groups, rows, BATCH * width), dout.dtype),
            pltpu.SemaphoreType.DMA((groups,)),
            pltpu.SemaphoreType.DMA((dests,)),
        ],
        compiler_params=pltpu.CompilerParams(vmem_limit_bytes=VMEM_LIMIT),
        cost_estimate=FREE,
        name="split",
    )(dout)


def attention_kernel(first, last, pairs, place_ref, *refs):
    pieces = len(pairs)
    d_refs = refs[:pieces]
    q_ref, o_ref, lse_ref, k_ref, v_ref = refs[pieces : pieces + 5]
    refs = refs[pieces + 5 :]
    if not first:
        dk_old, dv_old = refs[1:3]
        refs = refs[3:]
    dq_ref = refs[0]
    if last:
        terms_ref, d_ref, dk_ref, dv_ref = refs[1:]
    else:
        dk_ref, dv_ref, d_ref = refs[1:]
    step = pl.program_id(0)

    @pl.when(step == 0)
    def _():
        if first:
            dk_ref[...] = jnp.zeros_like(dk_ref)
            dv_ref[...] = jnp.zeros_like(dv_ref)
        else:
            dk_ref[...] = dk_old[...]
            dv_ref[...] = dv_old[...]
        rows = d_refs[0].shape[0]
        for index in range(pieces):
            distance = by_place(pairs[index], lax.rem(place_ref[0], 2))
            start = lax.rem(place_ref[0] ^ distance, pieces) * rows
            d_ref[pl.ds(pl.multiple_of(start, rows), rows), :] = d_refs[index][...]

    block, width = q_ref.shape
    columns = [slice(start, start + HEAD_SIZE) for start in range(0, width, HEAD_SIZE)]

    def stacked(array):
        return jnp.concatenate([array[:, c] for c in columns], axis=0)

    q, o, k, v = stacked(q_ref), stacked(o_ref), k_ref[...], v_ref[...]
    d = stacked(d_ref[pl.ds(pl.multiple_of(step * block, block), block), :])
    lse = jnp.concatenate([lse_ref[h : h + 1, :] for h in range(len(columns))], axis=1)
    scores = lax.dot_general(k, q, NT, preferred_element_type=jnp.float32) * FACTOR
    probs = jnp.exp(scores - lse)
    product = d.astype(jnp.float32) * o.astype(jnp.float32)
    high = product.astype(jnp.bfloat16)
    low = (product - high.astype(jnp.float32)).astype(jnp.bfloat16)
    minus = jnp.full(v.shape, -1.0, jnp.bfloat16)
    dprobs_less_delta = lax.dot_general(
        jnp.concatenate([v, minus, minus], axis=1),
        jnp.concatenate([d, high, low], axis=1),
        NT,
        preferred_element_type=jnp.float32,
    )
    dscores = (probs * dprobs_less_delta).astype(jnp.bfloat16)
    dq = lax.dot_general(dscores, k, TN, preferred_element_type=jnp.float32) * FACTOR
    for h, c in enumerate(columns):
        dq_ref[:, c] = dq[h * block : (h + 1) * block].astype(jnp.bfloat16)
    dk_ref[...] += jnp.dot(dscores, q, preferred_element_type=jnp.float32)
    dv_ref[...] += jnp.dot(probs.astype(jnp.bfloat16), d, preferred_element_type=jnp.float32)

    if last:

        @pl.when(step == pl.num_programs(0) - 1)
        def _():
            owned = terms_ref.shape[1] // 2
            for owner in range(terms_ref.shape[0]):
                rows = slice(owner * owned, (owner + 1) * owned)
                terms_ref[owner, :owned, :] = dk_ref[rows, :]
                terms_ref[owner, owned:, :] = dv_ref[rows, :]


def attention(pairs, place, arrived, first, owners, data, carried):
    queries, outputs, lse, k, v = data
    pieces = len(arrived)
    rows, width = arrived[0].shape
    heads = width // HEAD_SIZE
    keys = k.shape[0]
    block, steps = 2 * rows, pieces // 2

    def at(i, place):
        return (place[0] ^ by_place(pairs[0], lax.rem(place[0], 2))) // pieces * steps + i

    here = pl.BlockSpec((block, width), lambda i, place: (at(i, place), 0))
    whole = pl.BlockSpec((keys, HEAD_SIZE), lambda i, place: (0, 0))
    in_specs = [pl.BlockSpec((rows, width), lambda i, place: (0, 0))] * pieces + [
        here,
        here,
        pl.BlockSpec((heads, block), lambda i, place: (0, at(i, place))),
        whole,
        whole,
    ]
    operands = [place, *arrived, queries, outputs, lse, k, v]
    aliases = {}
    if not first:
        in_specs += [pl.BlockSpec(memory_space=pl.ANY), whole, whole]
        aliases = {len(operands): 0}
        operands += carried
    out_specs = [here]
    out_shape = [jax.ShapeDtypeStruct(queries.shape, jnp.bfloat16)]
    scratch = [pltpu.VMEM((pieces * rows, width), jnp.bfloat16)]
    if owners:
        terms = (owners, 2 * keys // owners, HEAD_SIZE)
        out_specs += [pl.BlockSpec(terms, lambda i, place: (0, 0, 0))]
        out_shape += [jax.ShapeDtypeStruct(terms, jnp.float32)]
        scratch += [pltpu.VMEM((keys, HEAD_SIZE), jnp.float32)] * 2
    else:
        out_specs += [whole, whole]
        out_shape += [jax.ShapeDtypeStruct((keys, HEAD_SIZE), jnp.float32)] * 2
    return pl.pallas_call(
        functools.partial(attention_kernel, first, owners > 0, pairs),
        grid_spec=pltpu.PrefetchScalarGridSpec(
            num_scalar_prefetch=1,
            grid=(steps,),
            in_specs=in_specs,
            out_specs=out_specs,
            scratch_shapes=scratch,
        ),
        out_shape=out_shape,
        input_output_aliases=aliases,
        compiler_params=pltpu.CompilerParams(
            vmem_limit_bytes=SMALL_LIMIT
        ),
        cost_estimate=FREE,
        name=f"sources_{pairs[0][0]}",
    )(*operands)


def sum_kernel(terms_ref, dk_ref, dv_ref):
    groups = KEY_VALUE_HEADS
    senders = terms_ref.shape[0] // groups
    owned = terms_ref.shape[1] // 2
    for group in range(groups):
        total = terms_ref[group * senders]
        for sender in range(1, senders):
            total = total + terms_ref[group * senders + sender]
        columns = slice(group * HEAD_SIZE, (group + 1) * HEAD_SIZE)
        dk_ref[:, columns] = (total[:owned] * FACTOR).astype(jnp.bfloat16)
        dv_ref[:, columns] = total[owned:].astype(jnp.bfloat16)


def swap(array, axis, size, bits):
    return lax.ppermute(array, axis, [(i, i ^ bits) for i in range(size)])


def after(array, *others):
    return lax.optimization_barrier((array,) + others)[0]


def own_group(keys, values, owners):
    owned = keys.shape[0]
    each = owners // KEY_VALUE_HEADS

    def kernel(k_ref, v_ref, out_ref):
        for group in range(KEY_VALUE_HEADS):
            columns = slice(group * HEAD_SIZE, (group + 1) * HEAD_SIZE)
            both = jnp.concatenate(
                [k_ref[:, columns].astype(jnp.float32), v_ref[:, columns].astype(jnp.float32)],
                axis=0,
            ).astype(keys.dtype)
            for index in range(each):
                out_ref[group * each + index] = both

    mine = pl.pallas_call(
        kernel,
        in_specs=[pl.BlockSpec(memory_space=pltpu.VMEM)] * 2,
        out_shape=jax.ShapeDtypeStruct((owners, 2 * owned, HEAD_SIZE), keys.dtype),
        name="pack_keys",
    )(keys, values)
    got = lax.all_to_all(mine, ("head", "ctx"), split_axis=0, concat_axis=0, tiled=True)
    return got[:, :owned].reshape(-1, HEAD_SIZE), got[:, owned:].reshape(-1, HEAD_SIZE)


def on_device(heads_axis, ctx_axis, queries, keys, values, outputs, dout, lse):
    owners = heads_axis * ctx_axis
    all_bases = batches(heads_axis)
    place = lax.axis_index("head").astype(jnp.int32).reshape(1)
    k, v = own_group(keys, values, owners)
    pieces = split(dout, heads_axis)
    data = (queries, outputs, lse, k, v)
    arrived = []

    def send(*gates):
        batch, index = divmod(len(arrived), BATCH)
        piece = after(pieces[len(arrived)], *gates)
        pairs = [
            (i, i ^ sent_distance(all_bases[batch], index, i % 2)) for i in range(heads_axis)
        ]
        arrived.append(lax.ppermute(piece, "head", pairs))

    def compute(start, count, carried):
        pairs = [
            tuple(base + i % BATCH for base in all_bases[i // BATCH])
            for i in range(start, start + count)
        ]
        return attention(
            pairs,
            place,
            arrived[start : start + count],
            start == 0,
            owners if start + count == heads_axis else 0,
            data,
            carried,
        )

    near = heads_axis // 2
    carried = []
    for place_in_order in range(heads_axis):
        gates = [arrived[place_in_order - 0]] if 0 and place_in_order >= 0 else []
        if 5 and place_in_order == near + 5:
            carried = compute(0, near, carried)
        if 5 and place_in_order >= near + 5:
            gates.append(carried[1])
        send(*gates)
    if not carried:
        carried = compute(0, near, carried)
    for start in range(near, heads_axis, 4):
        carried = compute(start, 4, carried)
    dq, terms = carried

    terms = lax.all_to_all(terms, ("head", "ctx"), split_axis=0, concat_axis=0, tiled=True)
    shape = jax.ShapeDtypeStruct(keys.shape, jnp.bfloat16)
    small = pltpu.CompilerParams(vmem_limit_bytes=8 * 1024 * 1024)
    dk, dv = pl.pallas_call(
        sum_kernel, out_shape=[shape, shape], compiler_params=small, name="sum_terms"
    )(terms)
    return dq, dk, dv


def solution(mesh):
    placed = (
        P("ctx", "head"),
        P(("head", "ctx"), None),
        P(("head", "ctx"), None),
        P("ctx", "head"),
        P(("ctx", "head"), None),
        P("head", "ctx"),
    )
    return jax.shard_map(
        functools.partial(on_device, mesh.shape["head"], mesh.shape["ctx"]),
        mesh=mesh,
        in_specs=placed,
        out_specs=(P("ctx", "head"), P(("head", "ctx"), None), P(("head", "ctx"), None)),
        check_vma=False,
    )
```
